1024 devices in a mesh: row: 16 (over z_lo, core), col: 16 (over y, x), layer: 4 (over z_hi).
Axes of the slice: x: 4, y: 4, z: 32 (z_hi: 4, z_lo: 8; z = z_hi * 8 + z_lo), core: 2. Of those that a mesh axis runs over, the one named last changes fastest.
Arguments:
- dens_blocks: bfloat16 [16, 16, 4, 16, 64, 128], P('row', 'col', 'layer'), may hold values from -0.0625 to 0.0625
- dens_ids: int32 [16, 16, 4, 16, 2], P('row', 'col', 'layer'), may hold values from 0 to 3, as said below
- ham_blocks: bfloat16 [16, 16, 4, 4, 64, 64], P('row', 'col', 'layer'), may hold values from -6 to 6
- ham_ids: int32 [16, 16, 4, 4, 1], P('row', 'col', 'layer'), may hold values from 0 to 1, as said below
- ovl_blocks: bfloat16 [16, 16, 4, 4, 64, 64], P('row', 'col', 'layer'), may hold values from -6 to 6
- ovl_ids: int32 [16, 16, 4, 4, 1], P('row', 'col', 'layer'), may hold values from 0 to 1, as said below
Outputs:
- dens_ham: float32 [256, 64, 2048], P(('row', 'layer'), None, 'col')
- dens_ovl: float32 [256, 64, 2048], P(('row', 'layer'), None, 'col')
The draws below stay inside these ranges and needn't reach their ends.
Inputs may be any that keep to these rules, and one draw needn't show every extreme that they name: `dens_ids`: the 2 ids of one block row of a density tile are distinct. `ham_ids`: the 1 ids of one block row of a Hamiltonian tile are distinct. `ovl_ids`: the 1 ids of one block row of a tile of S are distinct.
All inputs are finite; a program needn't handle non-finite values.
Results may differ from the reference program's by a relative error of at most 0.0003.
Values may be sent and summed in bfloat16 or wider, within the bound.
A program may use at most 32 MiB of HBM per device.

```python
import jax
import jax.numpy as jnp
from jax import lax

BLK = 64
KB = 4
CB = 2
SA = 2
SB = 1
RB = 16
N_ROW = 16
N_COL = 16
N_LAYER = 4


def distinct_picks(key, lead_shape, pool, picks):
    scores = jax.random.randint(key, lead_shape + (pool,), 0, 1 << 20) * pool + jnp.arange(pool, dtype=jnp.int32)
    order = jnp.argsort(scores, axis=-1)
    return order[..., :picks].astype(jnp.int32)


def draw_dens_ids(key, part):
    key = jax.random.fold_in(key, 11)
    return distinct_picks(key, (N_ROW, N_COL, N_LAYER, RB), KB, SA)


def draw_ham_ids(key, part):
    key = jax.random.fold_in(key, 23)
    return distinct_picks(key, (N_ROW, N_COL, N_LAYER, KB), CB, SB)


def draw_ovl_ids(key, part):
    key = jax.random.fold_in(key, 37)
    return distinct_picks(key, (N_ROW, N_COL, N_LAYER, KB), CB, SB)


def block_scale(key, dims, split, smallest, largest):
    def one(position, parts):
        heights = jax.random.uniform(jax.random.fold_in(jax.random.fold_in(key, 6), position), (parts,), jnp.float32, smallest / len(split), largest / len(split))
        return jnp.repeat(jnp.exp(heights), dims[position] // parts).reshape((-1,) + (1,) * (len(dims) - position - 1))

    gain = one(*split[0])
    for cut in split[1:]:
        gain = gain * one(*cut)
    return gain


def noise(stream_key, extent, width, reach, cuts=(), kind=jnp.bfloat16):
    gain = block_scale(stream_key, extent, cuts, -0.22, 0.18) if cuts else 1.0
    values = jax.random.normal(stream_key, extent, jnp.float32) * width * gain
    return jnp.minimum(jnp.maximum(values, -reach), reach).astype(kind)


def setup_inputs(seed: int = 0) -> dict:
    seeds = jax.random.split(jax.random.key(seed), 7)
    return {
        "dens_blocks": noise(seeds[0], (N_ROW, N_COL, N_LAYER, RB, BLK, SA * BLK), (SA * N_COL * N_LAYER * BLK) ** -0.5, 0.0625, ((0, 16), (1, 16), (2, 4))),
        "dens_ids": draw_dens_ids(jax.random.fold_in(seeds[6], 71), 0),
        "ham_blocks": noise(seeds[2], (N_ROW, N_COL, N_LAYER, KB, BLK, SB * BLK), 1.0, 6.0, ((0, 16), (1, 16), (2, 4))),
        "ham_ids": draw_ham_ids(jax.random.fold_in(seeds[6], 71), 0),
        "ovl_blocks": noise(seeds[4], (N_ROW, N_COL, N_LAYER, KB, BLK, SB * BLK), 1.0, 6.0, ((0, 16), (1, 16), (2, 4))),
        "ovl_ids": draw_ovl_ids(jax.random.fold_in(seeds[6], 71), 0),
    }


def densify(tile_vals, tile_ids, columns):
    onehot = (tile_ids[:, :, None] == jnp.arange(columns, dtype=jnp.int32)[None, None, :]).astype(jnp.float32)
    blocks = tile_vals.reshape(tile_vals.shape[0], tile_vals.shape[1], tile_ids.shape[1], tile_vals.shape[1]).astype(jnp.float32)
    dense_tile = jnp.einsum('kxbw,kbc->kxcw', blocks, onehot)
    return dense_tile.reshape(tile_vals.shape[0], tile_vals.shape[1], columns * tile_vals.shape[1]).astype(jnp.bfloat16)


def tile_product(dens_tile, dens_index, dense_tile):
    selected = dense_tile[dens_index]
    selected = selected.reshape(dens_index.shape[0], dens_index.shape[1] * dense_tile.shape[1], dense_tile.shape[2])
    return jnp.einsum('rxk,rkw->rxw', dens_tile.astype(jnp.float32), selected.astype(jnp.float32))


def reference(dens_blocks, dens_ids, ham_blocks, ham_ids, ovl_blocks, ovl_ids):
    grid_size = N_ROW
    flat = jax.vmap(jax.vmap(jax.vmap(lambda v, i: densify(v, i, CB))))
    ham_dense = flat(ham_blocks, ham_ids)
    ovl_dense = flat(ovl_blocks, ovl_ids)
    apply_all = jax.vmap(jax.vmap(tile_product))

    def one_row(row_at):
        dens_row = dens_blocks[row_at]
        ids_row = dens_ids[row_at]

        def one_col(col_at):
            source = (row_at + jnp.arange(grid_size, dtype=jnp.int32) - col_at) % grid_size
            ham_sel = ham_dense[source, col_at]
            ovl_sel = ovl_dense[source, col_at]
            first = jnp.sum(apply_all(dens_row, ids_row, ham_sel), axis=(0, 1))
            second = jnp.sum(apply_all(dens_row, ids_row, ovl_sel), axis=(0, 1))
            return first, second

        return lax.map(one_col, jnp.arange(grid_size, dtype=jnp.int32))

    first, second = lax.map(one_row, jnp.arange(grid_size, dtype=jnp.int32))

    def arrange(result):
        result = jnp.transpose(result, (0, 2, 3, 1, 4))
        return result.reshape(grid_size * RB, BLK, grid_size * CB * BLK)

    return arrange(first), arrange(second)
```

```python
import functools

import jax
import jax.numpy as jnp
from jax import lax
from jax.experimental import pallas as pl
from jax.experimental.pallas import tpu as pltpu
from jax.sharding import PartitionSpec as P

MESH = pl.DeviceIdType.MESH
BLK = 64
KB = 4
CB = 2
NX = 4
NY = 4
HEAD = 16
BODY = 4 * BLK
MSG = HEAD + BODY
CUT = HEAD + 2 * BLK
LANES = 2 * BLK


def swap_halves(x):
    return jnp.concatenate([x[:, BLK:], x[:, :BLK]], axis=1)


def kernel(
    n_row,
    n_layer,
    dens_ref,
    dids_ref,
    ham_ref,
    hids_ref,
    ovl_ref,
    oids_ref,
    outh_ref,
    outo_ref,
    amsg,
    abuf,
    bbuf,
    acc,
    send_sem,
    give_sem,
    first_sem,
    second_sem,
    ring_sem,
    pair_sem,
):
    n_col = NX * NY
    n_lo = n_row // 2
    n_z = n_lo * n_layer
    row, col, layer = lax.axis_index("row"), lax.axis_index("col"), lax.axis_index("layer")
    core = lax.rem(row, 2)
    z = layer * n_lo + row // 2
    x, y = lax.rem(col, NX), col // NX

    def at_z(other):
        return {"row": lax.rem(other, n_lo) * 2 + core, "col": col, "layer": other // n_lo}

    def at_xy(ox, oy):
        return {"row": row, "col": oy * NX + ox, "layer": layer}

    def at_layer(other):
        return {"row": row, "col": col, "layer": other}

    up, down = lax.rem(z + 1, n_z), lax.rem(z + n_z - 1, n_z)
    sibling = {"row": row + 1 - 2 * core, "col": col, "layer": layer}
    partners = [at_z(up), at_z(down), sibling]
    partners += [at_layer(lax.rem(layer + o, n_layer)) for o in range(1, n_layer)]
    partners += [at_xy(lax.rem(x + o, NX), y) for o in range(1, NX)]
    partners += [at_xy(x, lax.rem(y + o, NY)) for o in range(1, NY)]

    barrier = pltpu.get_barrier_semaphore()
    for partner in partners:
        pl.semaphore_signal(barrier, inc=1, device_id=partner, device_id_type=MESH)

    first_half = lax.broadcasted_iota(jnp.int32, (1, LANES), 1) < BLK
    pad = jnp.zeros((HEAD - 4, LANES), jnp.float32)

    def head(left, right):
        ids = jnp.where(first_half, left, right).astype(jnp.float32)
        return jnp.concatenate([ids, pad], axis=0).astype(jnp.bfloat16)

    dids = dids_ref[...]
    for q in range(n_layer):
        amsg[q, 0:HEAD, :] = head(dids[4 * q : 4 * q + 4, 0:1], dids[4 * q : 4 * q + 4, 1:2])
        amsg[q, HEAD:MSG, :] = dens_ref[4 * q : 4 * q + 4].reshape(BODY, LANES)
    abuf[layer, col] = amsg[layer]
    mine = z * 2 + core
    bbuf[mine, 0:HEAD, :] = head(hids_ref[...], oids_ref[...])
    bbuf[mine, HEAD:MSG, :] = jnp.concatenate(
        [ham_ref[...].reshape(BODY, BLK), ovl_ref[...].reshape(BODY, BLK)], axis=1
    )

    pl.semaphore_wait(barrier, len(partners))

    def copy(src, dst, sem, device):
        return pltpu.make_async_remote_copy(
            src_ref=src, dst_ref=dst, send_sem=send_sem, recv_sem=sem, device_id=device, device_id_type=MESH
        )

    sent = []

    def send(src, dst, sem, device):
        copy(src, dst, sem, device).start()
        sent.append((src, device))

    def received(ref, sem):
        copy(ref, ref, sem, sibling).wait_recv()

    halves = (pl.ds(0, CUT), pl.ds(CUT, MSG - CUT))

    def give_pieces():
        for o in range(1, n_layer):
            other = lax.rem(layer + o, n_layer)
            send(amsg.at[other], abuf.at[layer, col], give_sem.at[o], at_layer(other))

    def spread_x(l, j, half, sem):
        for o in range(1, NX):
            ref = abuf.at[l, j, halves[half]]
            send(ref, ref, sem(o), at_xy(lax.rem(x + o, NX), y))

    def spread_y(l, j, half, sem):
        for o in range(1, NY):
            ref = abuf.at[l, j, halves[half]]
            send(ref, ref, sem(o), at_xy(x, lax.rem(y + o, NY)))

    def first_phase(l, o):
        spread_x(l, col, 0, lambda k: first_sem.at[o, 0, k])
        spread_y(l, col, 1, lambda k: first_sem.at[o, 1, k])
        spread_y(l, col, 0, lambda k: second_sem.at[o, 0])
        spread_x(l, col, 1, lambda k: second_sem.at[o, 1])

    def second_phase(l, o):
        for k in range(1, max(NX, NY)):
            if k < NX:
                j = y * NX + lax.rem(x + NX - k, NX)
                received(abuf.at[l, j, halves[0]], first_sem.at[o, 0, k])
                spread_y(l, j, 0, lambda _: second_sem.at[o, 0])
            if k < NY:
                j = lax.rem(y + NY - k, NY) * NX + x
                received(abuf.at[l, j, halves[1]], first_sem.at[o, 1, k])
                spread_x(l, j, 1, lambda _: second_sem.at[o, 1])

    def gathered(l, o):
        received(abuf.at[l, pl.ds(0, NX * (NY - 1)), halves[0]], second_sem.at[o, 0])
        received(abuf.at[l, pl.ds(0, NY * (NX - 1)), halves[1]], second_sem.at[o, 1])

    def tile_of(plane):
        return lax.rem(plane + n_z, n_z) * 2 + core

    n_up, n_down = n_z // 2, n_z // 2 - 1

    def forward(s, way):
        ref = bbuf.at[tile_of(z - s if way == 0 else z + s)]
        send(ref, ref, ring_sem.at[way, s], at_z(up if way == 0 else down))

    def share(s, way):
        ref = bbuf.at[tile_of(z - s if way == 0 else z + s)]
        send(ref, ref, pair_sem.at[0], sibling)

    def arrived(s, way):
        ref = bbuf.at[tile_of(z - 1 - s if way == 0 else z + 1 + s)]
        received(ref, ring_sem.at[way, s])

    events = {}

    def other_layer(o):
        return lax.rem(layer + n_layer - o, n_layer)

    def take_piece(o):
        received(abuf.at[other_layer(o), col], give_sem.at[o])
        first_phase(other_layer(o), o)

    last = n_up - 1
    events.setdefault(min(1, last), []).append(lambda: second_phase(layer, 0))
    events.setdefault(min(5, last), []).append(lambda: (take_piece(1), take_piece(3)))
    events.setdefault(min(7, last), []).append(
        lambda: (second_phase(other_layer(1), 1), second_phase(other_layer(3), 3))
    )
    events.setdefault(min(10, last), []).append(lambda: take_piece(2))
    events.setdefault(min(12, last), []).append(lambda: second_phase(other_layer(2), 2))

    forward(0, 0)
    forward(0, 1)
    first_phase(layer, 0)
    give_pieces()
    share(0, 0)
    for s in range(n_up):
        arrived(s, 0)
        if s + 1 < n_up:
            forward(s + 1, 0)
        if s < n_down:
            arrived(s, 1)
            if s + 1 < n_down:
                forward(s + 1, 1)
        share(s + 1, 0)
        if s < n_down:
            share(s + 1, 1)
        for event in events.get(s, ()):
            event()
    for o in range(n_layer):
        gathered(other_layer(o), o)
    received(bbuf.at[pl.ds(0, n_z)], pair_sem.at[0])

    ones = jnp.ones((1, LANES), jnp.float32)
    left = jnp.where(first_half, ones, 0.0)
    lane_half = 1.0 - left

    def dense_a(l, j):
        ids = abuf[l, j, 0:HEAD, :].astype(jnp.float32)
        flip = swap_halves(ids)
        rows = []
        for r in range(4):
            data = abuf[l, j, HEAD + BLK * r : HEAD + BLK * (r + 1), :]
            turned = swap_halves(data)
            parts = []
            for base in (0.0, 2.0):
                want = lane_half + base
                keep = jnp.where(ids[r : r + 1] == want, 1.0, 0.0).astype(jnp.bfloat16)
                take = jnp.where(flip[r : r + 1] == want, 1.0, 0.0).astype(jnp.bfloat16)
                parts.append(data * keep + turned * take)
            rows.append(jnp.concatenate(parts, axis=1))
        return jnp.concatenate(rows, axis=0)

    def dense_b(f):
        ids = bbuf[f, 0:HEAD, :].astype(jnp.float32)
        flip = swap_halves(ids)
        rows = []
        for r in range(4):
            data = bbuf[f, HEAD + BLK * r : HEAD + BLK * (r + 1), :]
            turned = swap_halves(data)
            own, opp = ids[r : r + 1], flip[r : r + 1]

            def mask(which, value, side):
                return (jnp.where(which == value, 1.0, 0.0) * side).astype(jnp.bfloat16)

            ham = data * mask(own, 0.0, left) + turned * mask(opp, 1.0, lane_half)
            ovl = turned * mask(opp, 0.0, left) + data * mask(own, 1.0, lane_half)
            rows.append(jnp.concatenate([ham, ovl], axis=1))
        return jnp.concatenate(rows, axis=0)

    acc[...] = jnp.zeros_like(acc)

    def step(j, carry):
        for l in range(n_layer):
            group = lax.rem(row + j, n_row)
            f = l * n_row + lax.rem(group + n_row - col, n_row)
            acc[...] += jnp.dot(dense_a(l, j), dense_b(f), preferred_element_type=jnp.float32)
        return carry

    lax.fori_loop(0, n_col, step, 0)
    outh_ref[...] = acc[:, :LANES].reshape(4, BLK, LANES)
    outo_ref[...] = acc[:, LANES:].reshape(4, BLK, LANES)

    for ref, device in sent:
        copy(ref, ref, give_sem.at[0], device).wait_send()


def solution(mesh):
    n_row, n_col, n_layer = mesh.shape["row"], mesh.shape["col"], mesh.shape["layer"]
    n_z = n_row // 2 * n_layer

    def local(dens_blocks, dens_ids, ham_blocks, ham_ids, ovl_blocks, ovl_ids):
        out = jax.ShapeDtypeStruct((4, BLK, LANES), jnp.float32)
        return pl.pallas_call(
            functools.partial(kernel, n_row, n_layer),
            out_shape=(out, out),
            in_specs=[pl.BlockSpec(memory_space=pltpu.VMEM)] * 6,
            out_specs=[pl.BlockSpec(memory_space=pltpu.VMEM)] * 2,
            scratch_shapes=[
                pltpu.VMEM((n_layer, MSG, LANES), jnp.bfloat16),
                pltpu.VMEM((n_layer, n_col, MSG, LANES), jnp.bfloat16),
                pltpu.VMEM((n_z * 2, MSG, LANES), jnp.bfloat16),
                pltpu.VMEM((BODY, 2 * LANES), jnp.float32),
                pltpu.SemaphoreType.DMA,
                pltpu.SemaphoreType.DMA((n_layer,)),
                pltpu.SemaphoreType.DMA((n_layer, 2, max(NX, NY))),
                pltpu.SemaphoreType.DMA((n_layer, 2)),
                pltpu.SemaphoreType.DMA((2, n_z // 2)),
                pltpu.SemaphoreType.DMA((1,)),
            ],
            compiler_params=pltpu.CompilerParams(
                collective_id=0, has_side_effects=True, vmem_limit_bytes=40 * 1024 * 1024
            ),
        )(
            dens_blocks.reshape(4 * n_layer, BLK, LANES),
            dens_ids.reshape(4 * n_layer, 2),
            ham_blocks.reshape(KB, BLK, BLK),
            ham_ids.reshape(KB, 1),
            ovl_blocks.reshape(KB, BLK, BLK),
            ovl_ids.reshape(KB, 1),
        )

    tile = P("row", "col", "layer", None, None, None)
    ids = P("row", "col", "layer", None, None)
    out = P(("row", "layer"), None, "col")
    return jax.shard_map(
        local,
        mesh=mesh,
        in_specs=(tile, ids, tile, ids, tile, ids),
        out_specs=(out, out),
        check_vma=False,
    )
```

```python
import functools

import jax
import jax.numpy as jnp
from jax import lax
from jax.experimental import pallas as pl
from jax.experimental.pallas import tpu as pltpu
from jax.sharding import PartitionSpec as P

MESH = pl.DeviceIdType.MESH
BLK = 64
KB = 4
CB = 2
NX = 4
NY = 4
HEAD = 16
BODY = 4 * BLK
MSG = HEAD + BODY
CUT = HEAD + 2 * BLK
LANES = 2 * BLK


MSG_CUTS = (0, CUT, MSG)
EVENTS = (
    (-1, "give", 1, 0),
    (-1, "give", 3, 0),
    (-1, "first", 0, 0),
    (-1, "first", 0, 1),
    (0, "give", 1, 1),
    (0, "give", 3, 1),
    (1, "give", 2, 0),
    (2, "give", 2, 1),
    (2, "second", 0, 0),
    (2, "second", 0, 1),
    (4, "take", 1, 0),
    (4, "take", 3, 0),
    (5, "take", 1, 1),
    (5, "take", 3, 1),
    (6, "second", 1, 0),
    (6, "second", 3, 0),
    (7, "second", 1, 1),
    (7, "second", 3, 1),
    (8, "take", 2, 0),
    (9, "take", 2, 1),
    (9, "gathered", 0, 0),
    (9, "gathered", 0, 1),
    (9, "gathered", 1, 0),
    (9, "gathered", 1, 1),
    (9, "gathered", 3, 0),
    (9, "gathered", 3, 1),
    (9, "mul", 1, 3),
    (10, "mul", 3, 4),
    (11, "second", 2, 0),
    (11, "mul", 4, 5),
    (12, "second", 2, 1),
    (12, "mul", 5, 7),
    (13, "mul", 7, 9),
    (14, "gathered", 2, 0),
    (14, "gathered", 2, 1),
    (14, "mul", 9, 12),
    (15, "mul", 12, 15),
    (16, "mul", 15, 16),
)


def swap_halves(x):
    return pltpu.roll(x, BLK, 1)


def kernel(
    n_row,
    n_layer,
    dens_ref,
    dids_ref,
    ham_ref,
    hids_ref,
    ovl_ref,
    oids_ref,
    outh_ref,
    outo_ref,
    amsg,
    abuf,
    bbuf,
    acc,
    dids,
    hids,
    oids,
    ham,
    ovl,
    load_sem,
    send_sem,
    give_sem,
    first_sem,
    second_sem,
    ring_sem,
    pair_sem,
):
    n_col = NX * NY
    n_lo = n_row // 2
    n_z = n_lo * n_layer
    reach = n_z // 2
    row, col, layer = lax.axis_index("row"), lax.axis_index("col"), lax.axis_index("layer")
    core = lax.rem(row, 2)
    z = layer * n_lo + row // 2
    x, y = lax.rem(col, NX), col // NX
    way = 1 - 2 * core
    mine, theirs = core, 1 - core

    loads = [
        pltpu.make_async_copy(dids_ref, dids, load_sem.at[0]),
        pltpu.make_async_copy(hids_ref, hids, load_sem.at[1]),
        pltpu.make_async_copy(oids_ref, oids, load_sem.at[2]),
        pltpu.make_async_copy(ham_ref, ham, load_sem.at[3]),
        pltpu.make_async_copy(ovl_ref, ovl, load_sem.at[4]),
    ]
    loads += [
        pltpu.make_async_copy(
            dens_ref.at[pl.ds(BODY * q, BODY)], amsg.at[q, pl.ds(HEAD, BODY)], load_sem.at[5 + q]
        )
        for q in range(n_layer)
    ]
    loads.append(
        pltpu.make_async_copy(
            dens_ref.at[pl.ds(BODY * layer, BODY)],
            abuf.at[layer, col, pl.ds(HEAD, BODY)],
            load_sem.at[5 + n_layer],
        )
    )
    for load in loads:
        load.start()

    def at_z(other):
        return {"row": lax.rem(other, n_lo) * 2 + core, "col": col, "layer": other // n_lo}

    def at_xy(ox, oy):
        return {"row": row, "col": oy * NX + ox, "layer": layer}

    def at_layer(other):
        return {"row": row, "col": col, "layer": other}

    onward = at_z(lax.rem(z + way + n_z, n_z))
    behind_z = lax.rem(z - way + n_z, n_z)
    behind = at_z(behind_z)
    sibling = {"row": row + 1 - 2 * core, "col": col, "layer": layer}
    across = {"row": lax.rem(behind_z, n_lo) * 2 + 1 - core, "col": col, "layer": behind_z // n_lo}
    partners = [onward, behind, across, sibling]
    partners += [at_layer(lax.rem(layer + o, n_layer)) for o in range(1, n_layer)]
    partners += [at_xy(lax.rem(x + o, NX), y) for o in range(1, NX)]
    partners += [at_xy(x, lax.rem(y + o, NY)) for o in range(1, NY)]

    barrier = pltpu.get_barrier_semaphore()
    for partner in partners:
        pl.semaphore_signal(barrier, inc=1, device_id=partner, device_id_type=MESH)

    first_half = lax.broadcasted_iota(jnp.int32, (1, LANES), 1) < BLK

    def head(left, right):
        n = left.shape[1]
        at_row = lax.broadcasted_iota(jnp.int32, (HEAD, n), 0)
        at_lane = lax.broadcasted_iota(jnp.int32, (HEAD, n), 1)
        turn = lambda ids: jnp.sum(jnp.where(at_row == at_lane, ids, 0.0), axis=1, keepdims=True)
        return jnp.where(first_half, turn(left), turn(right))

    for load in loads:
        load.wait()
    whole = head(dids[0:1, :].astype(jnp.float32), dids[1:2, :].astype(jnp.float32))
    pad = jnp.zeros((HEAD - 4, LANES), jnp.float32)
    for q in range(n_layer):
        piece = jnp.concatenate([whole[4 * q : 4 * q + 4], pad], axis=0)
        amsg[q, 0:HEAD, :] = piece.astype(jnp.bfloat16)
    abuf[layer, col, 0:HEAD, :] = amsg[layer, 0:HEAD, :]
    own_tile = z * 2 + core
    bbuf[own_tile, 0:HEAD, :] = head(
        hids[...].astype(jnp.float32), oids[...].astype(jnp.float32)
    ).astype(jnp.bfloat16)
    bbuf[own_tile, HEAD:MSG, :] = jnp.concatenate([ham[...], ovl[...]], axis=1)
    acc[...] = jnp.zeros_like(acc)

    pl.semaphore_wait(barrier, len(partners))

    def copy(src, dst, sem, device):
        return pltpu.make_async_remote_copy(
            src_ref=src, dst_ref=dst, send_sem=send_sem, recv_sem=sem, device_id=device, device_id_type=MESH
        )

    sent = []

    def send(src, dst, sem, device):
        copy(src, dst, sem, device).start()
        sent.append((src, device))

    def received(ref, sem):
        copy(ref, ref, sem, sibling).wait_recv()

    halves = (pl.ds(0, CUT), pl.ds(CUT, MSG - CUT))

    def other_layer(o):
        return lax.rem(layer + n_layer - o, n_layer)

    def give(o, half):
        other = lax.rem(layer + o, n_layer)
        send(
            amsg.at[other, halves[half]],
            abuf.at[layer, col, halves[half]],
            give_sem.at[o, half],
            at_layer(other),
        )

    def spread(o, j, half, along_x, sem):
        ref = abuf.at[other_layer(o), j, halves[half]]
        for k in range(1, NX if along_x else NY):
            where = at_xy(lax.rem(x + k, NX), y) if along_x else at_xy(x, lax.rem(y + k, NY))
            send(ref, ref, sem(k), where)

    def first_phase(o, half):
        spread(o, col, half, half == 0, lambda k: first_sem.at[o, half, k])
        spread(o, col, half, half == 1, lambda k: second_sem.at[o, half])

    def second_phase(o, half):
        for k in range(1, NX if half == 0 else NY):
            if half == 0:
                j = y * NX + lax.rem(x + NX - k, NX)
            else:
                j = lax.rem(y + NY - k, NY) * NX + x
            received(abuf.at[other_layer(o), j, halves[half]], first_sem.at[o, half, k])
            spread(o, j, half, half == 1, lambda _: second_sem.at[o, half])

    def gathered(o, half):
        n = NX * (NY - 1) if half == 0 else NY * (NX - 1)
        received(abuf.at[other_layer(o), pl.ds(0, n), halves[half]], second_sem.at[o, half])

    def take(o, half):
        received(abuf.at[other_layer(o), col, halves[half]], give_sem.at[o, half])
        first_phase(o, half)

    steps = {"give": give, "take": take, "first": first_phase, "second": second_phase, "gathered": gathered}

    parts = [pl.ds(MSG_CUTS[k], MSG_CUTS[k + 1] - MSG_CUTS[k]) for k in range(len(MSG_CUTS) - 1)]

    def tile(s, which, direction):
        return lax.rem(z - direction * s + n_z, n_z) * 2 + which

    def pass_on(s, which, k, w, device):
        ref = bbuf.at[tile(s, which, way), parts[k]]
        send(ref, ref, ring_sem.at[s, w, k], device)

    def share(s, which, w):
        ref = bbuf.at[tile(s, which, way)]
        send(ref, ref, pair_sem.at[s, w], sibling)

    def arrived(s, which, k, w):
        received(bbuf.at[tile(s + 1, which, way), parts[k]], ring_sem.at[s, w, k])

    def shared(s, which, w):
        received(bbuf.at[tile(s, which, -way)], pair_sem.at[s, w])

    n_parts = len(parts)

    left = jnp.where(first_half, jnp.ones((1, LANES), jnp.float32), 0.0)
    lane_half = 1.0 - left

    def dense_a(l, j):
        ids = abuf[l, j, 0:HEAD, :].astype(jnp.float32)
        flip = swap_halves(ids)
        rows = []
        for r in range(4):
            data = abuf[l, j, HEAD + BLK * r : HEAD + BLK * (r + 1), :]
            turned = swap_halves(data)
            parts = []
            for base in (0.0, 2.0):
                want = lane_half + base
                keep = jnp.where(ids[r : r + 1] == want, 1.0, 0.0).astype(jnp.bfloat16)
                take = jnp.where(flip[r : r + 1] == want, 1.0, 0.0).astype(jnp.bfloat16)
                parts.append(data * keep + turned * take)
            rows.append(jnp.concatenate(parts, axis=1))
        return jnp.concatenate(rows, axis=0)

    def dense_b(f):
        ids = bbuf[f, 0:HEAD, :].astype(jnp.float32)
        flip = swap_halves(ids)
        rows = []
        for r in range(4):
            data = bbuf[f, HEAD + BLK * r : HEAD + BLK * (r + 1), :]
            turned = swap_halves(data)
            own, opp = ids[r : r + 1], flip[r : r + 1]

            def mask(which, value, side):
                return (jnp.where(which == value, 1.0, 0.0) * side).astype(jnp.bfloat16)

            ham = data * mask(own, 0.0, left) + turned * mask(opp, 1.0, lane_half)
            ovl = turned * mask(opp, 0.0, left) + data * mask(own, 1.0, lane_half)
            rows.append(jnp.concatenate([ham, ovl], axis=1))
        return jnp.concatenate(rows, axis=0)

    def multiply(tiles):
        lhs, rhs = [], []
        for f in tiles:
            j = lax.rem(lax.rem(f, n_row) + col + n_row - row, n_row)
            lhs.append(dense_a(f // n_row, j))
            rhs.append(dense_b(f))
        acc[...] += jnp.dot(
            jnp.concatenate(lhs, axis=1), jnp.concatenate(rhs, axis=0), preferred_element_type=jnp.float32
        )

    def multiply_at(s, carry):
        for w in range(2):
            shared(s, w, w)
        multiply([tile(s, 0, 1), tile(s, 1, 1), tile(s, 0, -1), tile(s, 1, -1)])
        return carry

    events = {}
    for at, kind, o, half in EVENTS:
        events.setdefault(at if at < 0 else min(at, reach), []).append((kind, o, half))

    def run_events(at):
        for kind, o, half in events.get(at, ()):
            if kind == "mul":
                lax.fori_loop(o, min(half, reach), multiply_at, 0)
            else:
                steps[kind](o, half)

    for k in range(n_parts):
        ref = bbuf.at[own_tile, parts[k]]
        send(ref, ref, ring_sem.at[0, mine, k], onward)
        send(ref, ref, ring_sem.at[0, mine, k], across)
    share(0, mine, 0)
    run_events(-1)
    for s in range(reach):
        last = s == reach - 1
        for w in range(1 if last else 2):
            for k in range(n_parts):
                arrived(s, mine if last else w, k, w)
                if s + 2 < reach:
                    pass_on(s + 1, w, k, w, onward)
        if s + 2 == reach:
            for k in range(n_parts):
                pass_on(s + 1, mine, k, 0, onward)
        for w in range(1 if last else 2):
            share(s + 1, mine if last else w, w)
        run_events(s)
    run_events(reach)
    shared(0, theirs, 0)
    shared(reach, theirs, 0)
    multiply([tile(0, 0, 1), tile(0, 1, 1), tile(reach, 0, 1), tile(reach, 1, 1)])
    outh_ref[...] = acc[:, :LANES].reshape(4, BLK, LANES)
    outo_ref[...] = acc[:, LANES:].reshape(4, BLK, LANES)
    for ref, device in sent:
        copy(ref, ref, give_sem.at[0, 0], device).wait_send()


def solution(mesh):
    n_row, n_col, n_layer = mesh.shape["row"], mesh.shape["col"], mesh.shape["layer"]
    n_z = n_row // 2 * n_layer

    def local(dens_blocks, dens_ids, ham_blocks, ham_ids, ovl_blocks, ovl_ids):
        out = jax.ShapeDtypeStruct((4, BLK, LANES), jnp.float32)
        return pl.pallas_call(
            functools.partial(kernel, n_row, n_layer),
            out_shape=(out, out),
            in_specs=[pl.BlockSpec(memory_space=pltpu.HBM)] * 6,
            out_specs=[pl.BlockSpec(memory_space=pltpu.VMEM)] * 2,
            scratch_shapes=[
                pltpu.VMEM((n_layer, MSG, LANES), jnp.bfloat16),
                pltpu.VMEM((n_layer, n_col, MSG, LANES), jnp.bfloat16),
                pltpu.VMEM((n_z * 2, MSG, LANES), jnp.bfloat16),
                pltpu.VMEM((BODY, 2 * LANES), jnp.float32),
                pltpu.VMEM((2, 4 * n_layer), jnp.int32),
                pltpu.VMEM((1, KB), jnp.int32),
                pltpu.VMEM((1, KB), jnp.int32),
                pltpu.VMEM((BODY, BLK), jnp.bfloat16),
                pltpu.VMEM((BODY, BLK), jnp.bfloat16),
                pltpu.SemaphoreType.DMA((6 + n_layer,)),
                pltpu.SemaphoreType.DMA,
                pltpu.SemaphoreType.DMA((n_layer, 2)),
                pltpu.SemaphoreType.DMA((n_layer, 2, max(NX, NY))),
                pltpu.SemaphoreType.DMA((n_layer, 2)),
                pltpu.SemaphoreType.DMA((n_z // 2, 2, len(MSG_CUTS) - 1)),
                pltpu.SemaphoreType.DMA((n_z // 2 + 1, 2)),
            ],
            compiler_params=pltpu.CompilerParams(
                collective_id=0, has_side_effects=True, vmem_limit_bytes=60 * 1024 * 1024
            ),
        )(
            dens_blocks.reshape(4 * n_layer * BLK, LANES),
            dens_ids.reshape(4 * n_layer, 2).T,
            ham_blocks.reshape(KB * BLK, BLK),
            ham_ids.reshape(1, KB),
            ovl_blocks.reshape(KB * BLK, BLK),
            ovl_ids.reshape(1, KB),
        )

    tile = P("row", "col", "layer", None, None, None)
    ids = P("row", "col", "layer", None, None)
    out = P(("row", "layer"), None, "col")
    return jax.shard_map(
        local,
        mesh=mesh,
        in_specs=(tile, ids, tile, ids, tile, ids),
        out_specs=(out, out),
        check_vma=False,
    )
```

```python
import functools

import jax
import jax.numpy as jnp
from jax import lax
from jax.experimental import pallas as pl
from jax.experimental.pallas import tpu as pltpu
from jax.sharding import PartitionSpec as P

MESH = pl.DeviceIdType.MESH
BLK = 64
KB = 4
CB = 2
NX = 4
NY = 4
HEAD = 16
BODY = 4 * BLK
MSG = HEAD + BODY
CUT = HEAD + 2 * BLK
LANES = 2 * BLK


MSG_CUTS = (0, CUT, MSG)
EVENTS = (
    (-1, "give", 1, 0),
    (-1, "give", 3, 0),
    (-1, "first", 0, 0),
    (-1, "first", 0, 1),
    (0, "give", 1, 1),
    (0, "give", 3, 1),
    (1, "give", 2, 0),
    (2, "give", 2, 1),
    (2, "second", 0, 0),
    (2, "second", 0, 1),
    (4, "take", 1, 0),
    (4, "take", 3, 0),
    (5, "take", 1, 1),
    (5, "take", 3, 1),
    (6, "second", 1, 0),
    (6, "second", 3, 0),
    (7, "second", 1, 1),
    (7, "second", 3, 1),
    (8, "take", 2, 0),
    (9, "take", 2, 1),
    (9, "gathered", 0, 0),
    (9, "gathered", 0, 1),
    (10, "gathered", 1, 0),
    (10, "gathered", 1, 1),
    (10, "gathered", 3, 0),
    (10, "gathered", 3, 1),
    (10, "mul", 1, 3),
    (11, "second", 2, 0),
    (11, "mul", 3, 4),
    (12, "second", 2, 1),
    (12, "mul", 4, 6),
    (13, "mul", 6, 9),
    (14, "gathered", 2, 0),
    (14, "gathered", 2, 1),
    (14, "mul", 9, 11),
    (15, "mul", 11, 13),
    (16, "mul", 13, 16),
)


def swap_halves(x):
    return pltpu.roll(x, BLK, 1)


def kernel(
    n_row,
    n_layer,
    dens_ref,
    dids_ref,
    ham_ref,
    hids_ref,
    ovl_ref,
    oids_ref,
    outh_ref,
    outo_ref,
    amsg,
    abuf,
    bbuf,
    acc,
    dids,
    hids,
    oids,
    ham,
    ovl,
    load_sem,
    send_sem,
    give_sem,
    first_sem,
    second_sem,
    ring_sem,
    pair_sem,
):
    n_col = NX * NY
    n_lo = n_row // 2
    n_z = n_lo * n_layer
    reach = n_z // 2
    row, col, layer = lax.axis_index("row"), lax.axis_index("col"), lax.axis_index("layer")
    core = lax.rem(row, 2)
    z = layer * n_lo + row // 2
    x, y = lax.rem(col, NX), col // NX
    way = 1 - 2 * core
    mine, theirs = core, 1 - core

    loads = [
        pltpu.make_async_copy(dids_ref, dids, load_sem.at[0]),
        pltpu.make_async_copy(hids_ref, hids, load_sem.at[1]),
        pltpu.make_async_copy(oids_ref, oids, load_sem.at[2]),
        pltpu.make_async_copy(ham_ref, ham, load_sem.at[3]),
        pltpu.make_async_copy(ovl_ref, ovl, load_sem.at[4]),
    ]
    loads += [
        pltpu.make_async_copy(
            dens_ref.at[pl.ds(BODY * q, BODY)], amsg.at[q, pl.ds(HEAD, BODY)], load_sem.at[5 + q]
        )
        for q in range(n_layer)
    ]
    loads.append(
        pltpu.make_async_copy(
            dens_ref.at[pl.ds(BODY * layer, BODY)],
            abuf.at[layer, col, pl.ds(HEAD, BODY)],
            load_sem.at[5 + n_layer],
        )
    )
    for load in loads:
        load.start()

    def at_z(other):
        return {"row": lax.rem(other, n_lo) * 2 + core, "col": col, "layer": other // n_lo}

    def at_xy(ox, oy):
        return {"row": row, "col": oy * NX + ox, "layer": layer}

    def at_layer(other):
        return {"row": row, "col": col, "layer": other}

    onward = at_z(lax.rem(z + way + n_z, n_z))
    behind_z = lax.rem(z - way + n_z, n_z)
    behind = at_z(behind_z)
    sibling = {"row": row + 1 - 2 * core, "col": col, "layer": layer}
    across = {"row": lax.rem(behind_z, n_lo) * 2 + 1 - core, "col": col, "layer": behind_z // n_lo}
    partners = [onward, behind, across, sibling]
    partners += [at_layer(lax.rem(layer + o, n_layer)) for o in range(1, n_layer)]
    partners += [at_xy(lax.rem(x + o, NX), y) for o in range(1, NX)]
    partners += [at_xy(x, lax.rem(y + o, NY)) for o in range(1, NY)]

    barrier = pltpu.get_barrier_semaphore()
    for partner in partners:
        pl.semaphore_signal(barrier, inc=1, device_id=partner, device_id_type=MESH)

    first_half = lax.broadcasted_iota(jnp.int32, (1, LANES), 1) < BLK

    def head(left, right):
        n = left.shape[1]
        at_row = lax.broadcasted_iota(jnp.int32, (HEAD, n), 0)
        at_lane = lax.broadcasted_iota(jnp.int32, (HEAD, n), 1)
        turn = lambda ids: jnp.sum(jnp.where(at_row == at_lane, ids, 0.0), axis=1, keepdims=True)
        return jnp.where(first_half, turn(left), turn(right))

    for load in loads:
        load.wait()
    whole = head(dids[0:1, :].astype(jnp.float32), dids[1:2, :].astype(jnp.float32))
    pad = jnp.zeros((HEAD - 4, LANES), jnp.float32)
    for q in range(n_layer):
        piece = jnp.concatenate([whole[4 * q : 4 * q + 4], pad], axis=0)
        amsg[q, 0:HEAD, :] = piece.astype(jnp.bfloat16)
    abuf[layer, col, 0:HEAD, :] = amsg[layer, 0:HEAD, :]
    own_tile = z * 2 + core
    bbuf[own_tile, 0:HEAD, :] = head(
        hids[...].astype(jnp.float32), oids[...].astype(jnp.float32)
    ).astype(jnp.bfloat16)
    bbuf[own_tile, HEAD:MSG, :] = jnp.concatenate([ham[...], ovl[...]], axis=1)
    acc[...] = jnp.zeros_like(acc)

    pl.semaphore_wait(barrier, len(partners))

    def copy(src, dst, sem, device):
        return pltpu.make_async_remote_copy(
            src_ref=src, dst_ref=dst, send_sem=send_sem, recv_sem=sem, device_id=device, device_id_type=MESH
        )

    sent = []

    def send(src, dst, sem, device):
        copy(src, dst, sem, device).start()
        sent.append((src, device))

    def received(ref, sem):
        copy(ref, ref, sem, sibling).wait_recv()

    halves = (pl.ds(0, CUT), pl.ds(CUT, MSG - CUT))

    def other_layer(o):
        return lax.rem(layer + n_layer - o, n_layer)

    def give(o, half):
        other = lax.rem(layer + o, n_layer)
        send(
            amsg.at[other, halves[half]],
            abuf.at[layer, col, halves[half]],
            give_sem.at[o, half],
            at_layer(other),
        )

    def spread(o, j, half, along_x, sem):
        ref = abuf.at[other_layer(o), j, halves[half]]
        for k in range(1, NX if along_x else NY):
            where = at_xy(lax.rem(x + k, NX), y) if along_x else at_xy(x, lax.rem(y + k, NY))
            send(ref, ref, sem(k), where)

    def first_phase(o, half):
        spread(o, col, half, half == 0, lambda k: first_sem.at[o, half, k])
        spread(o, col, half, half == 1, lambda k: second_sem.at[o, half])

    def second_phase(o, half):
        for k in range(1, NX if half == 0 else NY):
            if half == 0:
                j = y * NX + lax.rem(x + NX - k, NX)
            else:
                j = lax.rem(y + NY - k, NY) * NX + x
            received(abuf.at[other_layer(o), j, halves[half]], first_sem.at[o, half, k])
            spread(o, j, half, half == 1, lambda _: second_sem.at[o, half])

    def gathered(o, half):
        n = NX * (NY - 1) if half == 0 else NY * (NX - 1)
        received(abuf.at[other_layer(o), pl.ds(0, n), halves[half]], second_sem.at[o, half])

    def take(o, half):
        received(abuf.at[other_layer(o), col, halves[half]], give_sem.at[o, half])
        first_phase(o, half)

    steps = {"give": give, "take": take, "first": first_phase, "second": second_phase, "gathered": gathered}

    parts = [pl.ds(MSG_CUTS[k], MSG_CUTS[k + 1] - MSG_CUTS[k]) for k in range(len(MSG_CUTS) - 1)]

    def tile(s, which, direction):
        return lax.rem(z - direction * s + n_z, n_z) * 2 + which

    def pass_on(s, which, k, w, device):
        ref = bbuf.at[tile(s, which, way), parts[k]]
        send(ref, ref, ring_sem.at[s, w, k], device)

    def share(s, which, w):
        ref = bbuf.at[tile(s, which, way)]
        send(ref, ref, pair_sem.at[s, w], sibling)

    def arrived(s, which, k, w):
        received(bbuf.at[tile(s + 1, which, way), parts[k]], ring_sem.at[s, w, k])

    def shared(s, which, w):
        received(bbuf.at[tile(s, which, -way)], pair_sem.at[s, w])

    n_parts = len(parts)

    left = jnp.where(first_half, jnp.ones((1, LANES), jnp.float32), 0.0)
    lane_half = 1.0 - left

    def dense_a(l, j):
        ids = abuf[l, j, 0:HEAD, :].astype(jnp.float32)
        flip = swap_halves(ids)
        rows = []
        for r in range(4):
            data = abuf[l, j, HEAD + BLK * r : HEAD + BLK * (r + 1), :]
            turned = swap_halves(data)
            parts = []
            for base in (0.0, 2.0):
                want = lane_half + base
                keep = jnp.where(ids[r : r + 1] == want, 1.0, 0.0).astype(jnp.bfloat16)
                take = jnp.where(flip[r : r + 1] == want, 1.0, 0.0).astype(jnp.bfloat16)
                parts.append(data * keep + turned * take)
            rows.append(jnp.concatenate(parts, axis=1))
        return jnp.concatenate(rows, axis=0)

    def dense_b(f):
        ids = bbuf[f, 0:HEAD, :].astype(jnp.float32)
        flip = swap_halves(ids)
        rows = []
        for r in range(4):
            data = bbuf[f, HEAD + BLK * r : HEAD + BLK * (r + 1), :]
            turned = swap_halves(data)
            own, opp = ids[r : r + 1], flip[r : r + 1]

            def mask(which, value, side):
                return (jnp.where(which == value, 1.0, 0.0) * side).astype(jnp.bfloat16)

            ham = data * mask(own, 0.0, left) + turned * mask(opp, 1.0, lane_half)
            ovl = turned * mask(opp, 0.0, left) + data * mask(own, 1.0, lane_half)
            rows.append(jnp.concatenate([ham, ovl], axis=1))
        return jnp.concatenate(rows, axis=0)

    def multiply(tiles):
        lhs, rhs = [], []
        for f in tiles:
            j = lax.rem(lax.rem(f, n_row) + col + n_row - row, n_row)
            lhs.append(dense_a(f // n_row, j))
            rhs.append(dense_b(f))
        acc[...] += jnp.dot(
            jnp.concatenate(lhs, axis=1), jnp.concatenate(rhs, axis=0), preferred_element_type=jnp.float32
        )

    def multiply_at(s, carry):
        for w in range(2):
            shared(s, w, w)
        multiply([tile(s, 0, 1), tile(s, 1, 1), tile(s, 0, -1), tile(s, 1, -1)])
        return carry

    events = {}
    for at, kind, o, half in EVENTS:
        events.setdefault(at if at < 0 else min(at, reach), []).append((kind, o, half))

    def run_events(at):
        for kind, o, half in events.get(at, ()):
            if kind == "mul":
                lax.fori_loop(o, min(half, reach), multiply_at, 0)
            else:
                steps[kind](o, half)

    for k in range(n_parts):
        ref = bbuf.at[own_tile, parts[k]]
        send(ref, ref, ring_sem.at[0, mine, k], onward)
        send(ref, ref, ring_sem.at[0, mine, k], across)
    share(0, mine, 0)
    run_events(-1)
    for s in range(reach):
        last = s == reach - 1
        for w in range(1 if last else 2):
            for k in range(n_parts):
                arrived(s, mine if last else w, k, w)
                if s + 2 < reach:
                    pass_on(s + 1, w, k, w, onward)
        if s + 2 == reach:
            for k in range(n_parts):
                pass_on(s + 1, mine, k, 0, onward)
        for w in range(1 if last else 2):
            share(s + 1, mine if last else w, w)
        run_events(s)
    run_events(reach)
    shared(0, theirs, 0)
    shared(reach, theirs, 0)
    multiply([tile(0, 0, 1), tile(0, 1, 1), tile(reach, 0, 1), tile(reach, 1, 1)])
    outh_ref[...] = acc[:, :LANES].reshape(4, BLK, LANES)
    outo_ref[...] = acc[:, LANES:].reshape(4, BLK, LANES)
    for ref, device in sent:
        copy(ref, ref, give_sem.at[0, 0], device).wait_send()


def solution(mesh):
    n_row, n_col, n_layer = mesh.shape["row"], mesh.shape["col"], mesh.shape["layer"]
    n_z = n_row // 2 * n_layer

    def local(dens_blocks, dens_ids, ham_blocks, ham_ids, ovl_blocks, ovl_ids):
        out = jax.ShapeDtypeStruct((4, BLK, LANES), jnp.float32)
        return pl.pallas_call(
            functools.partial(kernel, n_row, n_layer),
            out_shape=(out, out),
            in_specs=[pl.BlockSpec(memory_space=pltpu.HBM)] * 6,
            out_specs=[pl.BlockSpec(memory_space=pltpu.VMEM)] * 2,
            scratch_shapes=[
                pltpu.VMEM((n_layer, MSG, LANES), jnp.bfloat16),
                pltpu.VMEM((n_layer, n_col, MSG, LANES), jnp.bfloat16),
                pltpu.VMEM((n_z * 2, MSG, LANES), jnp.bfloat16),
                pltpu.VMEM((BODY, 2 * LANES), jnp.float32),
                pltpu.VMEM((2, 4 * n_layer), jnp.int32),
                pltpu.VMEM((1, KB), jnp.int32),
                pltpu.VMEM((1, KB), jnp.int32),
                pltpu.VMEM((BODY, BLK), jnp.bfloat16),
                pltpu.VMEM((BODY, BLK), jnp.bfloat16),
                pltpu.SemaphoreType.DMA((6 + n_layer,)),
                pltpu.SemaphoreType.DMA,
                pltpu.SemaphoreType.DMA((n_layer, 2)),
                pltpu.SemaphoreType.DMA((n_layer, 2, max(NX, NY))),
                pltpu.SemaphoreType.DMA((n_layer, 2)),
                pltpu.SemaphoreType.DMA((n_z // 2, 2, len(MSG_CUTS) - 1)),
                pltpu.SemaphoreType.DMA((n_z // 2 + 1, 2)),
            ],
            compiler_params=pltpu.CompilerParams(
                collective_id=0, has_side_effects=True, vmem_limit_bytes=60 * 1024 * 1024
            ),
        )(
            dens_blocks.reshape(4 * n_layer * BLK, LANES),
            dens_ids.reshape(4 * n_layer, 2).T,
            ham_blocks.reshape(KB * BLK, BLK),
            ham_ids.reshape(1, KB),
            ovl_blocks.reshape(KB * BLK, BLK),
            ovl_ids.reshape(1, KB),
        )

    tile = P("row", "col", "layer", None, None, None)
    ids = P("row", "col", "layer", None, None)
    out = P(("row", "layer"), None, "col")
    return jax.shard_map(
        local,
        mesh=mesh,
        in_specs=(tile, ids, tile, ids, tile, ids),
        out_specs=(out, out),
        check_vma=False,
    )
```
